32 devices in a mesh: ctx: 8 (over z, x), dp: 4 (over y, core).
Axes of the slice: x: 2, y: 2, z: 4, core: 2. Of those that a mesh axis runs over, the one named last changes fastest.
Arguments:
- query: bfloat16 [4, 1024, 1024], P('dp', 'ctx'), may hold values from -6 to 6
- key_in: bfloat16 [4, 1024, 1024], P('dp', 'ctx'), may hold values from -6 to 6
- value: bfloat16 [4, 1024, 1024], P('dp', 'ctx'), may hold values from -6 to 6
- cotangent: bfloat16 [4, 1024, 1024], P('dp', 'ctx'), may hold values from -6 to 6
- filters: bfloat16 [32, 1024], P('ctx'), may hold values from -0.1875 to 0.1875
Outputs:
- output: bfloat16 [4, 1024, 1024], P('dp', 'ctx')
- grad_query: bfloat16 [4, 1024, 1024], P('dp', 'ctx')
- grad_key: bfloat16 [4, 1024, 1024], P('dp', 'ctx')
- grad_value: bfloat16 [4, 1024, 1024], P('dp', 'ctx')
- grad_filter: float32 [32, 1024], P('ctx', 'dp')
The draws below stay inside these ranges and needn't reach their ends.
All inputs are finite; a program needn't handle non-finite values.
Results may differ from the reference program's by a relative error of at most 0.0058.
Values may be sent and summed in bfloat16 or wider, within the bound.
A program may use at most 64 MiB of HBM per device.

```python
import math
import jax
import jax.numpy as jnp
from jax import lax

C = 1024
CPG = 32
BLK = 256
LENGTH = 1024
BATCH = 4
GROUPS = 32


def steps_of(key, extent, pieces, least, largest):
    factor_of, own = 1.0, jax.random.fold_in(key, 6)
    for axis_at, parts in pieces:
        heights = jnp.exp(jax.random.uniform(jax.random.fold_in(own, axis_at), (parts,), jnp.float32, least / len(pieces), largest / len(pieces)))
        factor_of = factor_of * jnp.repeat(heights, extent[axis_at] // parts).reshape([-1 if axis == axis_at else 1 for axis in range(len(extent))])
    return factor_of


def gaussian(rng, dims, deviation, limit, cuts=(), held_as=jnp.bfloat16):
    loudness = steps_of(rng, dims, cuts, -0.22, 0.18) if cuts else 1.0
    values = jax.random.normal(rng, dims, jnp.float32) * deviation * loudness
    return jnp.minimum(jnp.maximum(values, -limit), limit).astype(held_as)


def setup_inputs(seed: int = 0) -> dict:
    key_list = jax.random.split(jax.random.key(seed), 6)
    return {
        "query": gaussian(key_list[0], (BATCH, LENGTH, C), 1.0, 6.0, ((0, 4), (1, 8))),
        "key_in": gaussian(key_list[1], (BATCH, LENGTH, C), 1.0, 6.0, ((0, 4), (1, 8))),
        "value": gaussian(key_list[2], (BATCH, LENGTH, C), 1.0, 6.0, ((0, 4), (1, 8))),
        "cotangent": gaussian(key_list[3], (BATCH, LENGTH, C), 1.0, 6.0, ((0, 4), (1, 8))),
        "filters": gaussian(key_list[4], (GROUPS, LENGTH), LENGTH ** -0.5, 0.1875, ((0, 8),)),
    }


def to_blocks(values, blocksize):
    seqcount, length, width = values.shape
    groups = width // CPG
    nblocks = length // blocksize
    arranged = values.reshape(seqcount, nblocks, blocksize, groups, CPG).transpose(3, 2, 1, 0, 4)
    return arranged.reshape(groups, blocksize, nblocks, seqcount * CPG)

def from_blocks(arranged, seqcount):
    groups, blocksize, nblocks, columns = arranged.shape
    values = arranged.reshape(groups, blocksize, nblocks, seqcount, CPG).transpose(3, 2, 1, 0, 4)
    return values.reshape(seqcount, nblocks * blocksize, groups * CPG)

def toeplitz_blocks(filters_local, blocksize):
    groups, length = filters_local.shape
    nblocks = length // blocksize
    extended = jnp.concatenate([jnp.zeros((groups, blocksize - 1), filters_local.dtype), filters_local], axis=1)
    matrices = []
    for offset in range(nblocks):
        window = extended[:, offset * blocksize:offset * blocksize + 2 * blocksize - 1]
        tiled = jnp.tile(window[:, ::-1], (1, blocksize))
        strided = tiled[:, blocksize - 1:blocksize - 1 + blocksize * (2 * blocksize - 2)]
        matrices.append(strided.reshape(groups, blocksize, 2 * blocksize - 2)[:, :, :blocksize])
    return matrices

def conv_forward(matrices, signal):
    groups, blocksize, nblocks, columns = signal.shape
    result = jnp.zeros(signal.shape, jnp.float32)
    for offset, matrix in enumerate(matrices):
        inputs = signal[:, :, :nblocks - offset].reshape(groups, blocksize, (nblocks - offset) * columns)
        partial_out = jnp.einsum('gab,gbw->gaw', matrix.astype(jnp.float32), inputs.astype(jnp.float32))
        partial_out = partial_out.reshape(groups, blocksize, nblocks - offset, columns)
        result = result + jnp.pad(partial_out, ((0, 0), (0, 0), (offset, 0), (0, 0)))
    return result

def conv_adjoint(matrices, grads):
    groups, blocksize, nblocks, columns = grads.shape
    result = jnp.zeros(grads.shape, jnp.float32)
    for offset, matrix in enumerate(matrices):
        outgrad = grads[:, :, offset:].reshape(groups, blocksize, (nblocks - offset) * columns)
        partial_in = jnp.einsum('gab,gaw->gbw', matrix.astype(jnp.float32), outgrad.astype(jnp.float32))
        partial_in = partial_in.reshape(groups, blocksize, nblocks - offset, columns)
        result = result + jnp.pad(partial_in, ((0, 0), (0, 0), (0, offset), (0, 0)))
    return result

def skew_sums(square):
    groups, blocksize, second = square.shape
    padded = jnp.concatenate([square, jnp.zeros_like(square)], axis=2)
    padded = padded.reshape(groups, 2 * blocksize * blocksize)[:, :blocksize * (2 * blocksize - 1)]
    return padded.reshape(groups, blocksize, 2 * blocksize - 1).sum(axis=1)

def filter_terms(grads, signal):
    groups, blocksize, nblocks, columns = signal.shape
    total = jnp.zeros((groups, nblocks * blocksize + blocksize - 1), jnp.float32)
    for offset in range(nblocks):
        outgrad = grads[:, :, offset:].reshape(groups, blocksize, (nblocks - offset) * columns)
        earlier = signal[:, ::-1, :nblocks - offset].reshape(groups, blocksize, (nblocks - offset) * columns)
        flipped = jnp.einsum('gaw,gbw->gab', outgrad.astype(jnp.float32), earlier.astype(jnp.float32))
        total = total + jnp.pad(skew_sums(flipped), ((0, 0), (offset * blocksize, (nblocks - 1 - offset) * blocksize)))
    return total[:, blocksize - 1:]

def reference(query, key_in, value, cotangent, filters):
    mixed = (key_in.astype(jnp.float32) * value.astype(jnp.float32)).astype(jnp.bfloat16)
    gradin = (cotangent.astype(jnp.float32) * query.astype(jnp.float32)).astype(jnp.bfloat16)
    ngroups = C // CPG

    def split(values):
        return values.reshape(BATCH, LENGTH, ngroups, CPG).transpose(2, 0, 1, 3)

    def one_group(operands):
        filt, mixed_group, grad_group = operands
        matrices = toeplitz_blocks(filt[None, :].astype(jnp.float32), BLK)
        signal = to_blocks(mixed_group, BLK)
        grads = to_blocks(grad_group, BLK)
        conv_group = from_blocks(conv_forward(matrices, signal).astype(jnp.bfloat16), BATCH)
        adjoint_group = from_blocks(conv_adjoint(matrices, grads).astype(jnp.bfloat16), BATCH)
        lag_sums = filter_terms(grads, signal)
        return (conv_group, adjoint_group, lag_sums[0])
    conv_all, adjoint_all, lag_all = lax.map(one_group, (filters, split(mixed), split(gradin)))
    conv = conv_all.transpose(1, 2, 0, 3).reshape(BATCH, LENGTH, C)
    adjoint = adjoint_all.transpose(1, 2, 0, 3).reshape(BATCH, LENGTH, C)
    output = (query.astype(jnp.float32) * conv.astype(jnp.float32)).astype(jnp.bfloat16)
    grad_query = (cotangent.astype(jnp.float32) * conv.astype(jnp.float32)).astype(jnp.bfloat16)
    grad_key = (adjoint.astype(jnp.float32) * value.astype(jnp.float32)).astype(jnp.bfloat16)
    grad_value = (adjoint.astype(jnp.float32) * key_in.astype(jnp.float32)).astype(jnp.bfloat16)
    scale_factor = 1.0 / math.sqrt(BATCH * LENGTH * CPG)
    grad_filter = lag_all * jnp.float32(scale_factor)
    return (output, grad_query, grad_key, grad_value, grad_filter)
```

```python
import functools
import math

import jax
import jax.numpy as jnp
from jax import lax
from jax.experimental import pallas as pl
from jax.experimental.pallas import tpu as pltpu
from jax.sharding import PartitionSpec as P

CPG = 32
MESH = pl.DeviceIdType.MESH
F32 = jnp.float32
BF16 = jnp.bfloat16


def dot(a, b, contract=((1,), (0,))):
    return lax.dot_general(a, b, (contract, ((), ())), preferred_element_type=F32)


def kernel(
    n, ndp, scale,
    q_ref, k_ref, v_ref, ct_ref, f_ref,
    conv_ref, adj_ref, gf_ref,
    send, recv, strips, masked, retc, reta, backc, backa, lhs, rhs, lags, gsend, grecv,
    send_sem, recv_sem, csend_sem, crecv_sem, asend_sem, arecv_sem, gsend_sem, grecv_sem,
):
    me = lax.axis_index("ctx")
    row = lax.axis_index("dp")
    piece, channels = q_ref.shape
    width = channels // n
    groups, length = f_ref.shape
    part = length // ndp

    barrier = pltpu.get_barrier_semaphore()
    for step in range(1, n):
        pl.semaphore_signal(
            barrier, inc=1, device_id={"ctx": lax.rem(me + step, n)}, device_id_type=MESH
        )
    for step in range(1, ndp):
        pl.semaphore_signal(
            barrier, inc=1, device_id={"dp": lax.rem(row + step, ndp)}, device_id_type=MESH
        )

    at_row = lax.broadcasted_iota(jnp.int32, (piece, piece), 0)
    at_col = lax.broadcasted_iota(jnp.int32, (piece, piece), 1)
    flip = jnp.where(at_row + at_col == piece - 1, 1.0, 0.0).astype(BF16)

    mixed = (k_ref[...].astype(F32) * v_ref[...].astype(F32)).astype(BF16)
    turned = dot(flip, mixed).astype(BF16)
    gradin = (ct_ref[...].astype(F32) * q_ref[...].astype(F32)).astype(BF16)
    for owner in range(n):
        span = slice(owner * width, (owner + 1) * width)
        send[owner, :, :width] = turned[:, span]
        send[owner, :, width:] = gradin[:, span]
    pl.semaphore_wait(barrier, n - 1 + ndp - 1)

    def outward(step):
        owner = lax.rem(me + step, n)
        return pltpu.make_async_remote_copy(
            src_ref=send.at[owner], dst_ref=recv.at[me],
            send_sem=send_sem.at[owner], recv_sem=recv_sem.at[me],
            device_id={"ctx": owner}, device_id_type=MESH,
        )

    def inward(source):
        return pltpu.make_async_remote_copy(
            src_ref=send.at[source], dst_ref=recv.at[source],
            send_sem=send_sem.at[source], recv_sem=recv_sem.at[source],
            device_id={"ctx": source}, device_id_type=MESH,
        )

    for step in range(1, n):
        outward(step).start()
    recv[me] = send[me]

    filters = f_ref[...].astype(F32)
    padded = jnp.concatenate([filters, jnp.zeros((groups, piece), F32)], axis=1)
    for g in range(groups):
        spread = jnp.broadcast_to(padded[g : g + 1], (piece, length + piece))
        strip = pltpu.roll(spread, 0, 1, stride=1, stride_axis=0).astype(BF16)
        strips[g, :piece] = strip[:, :length]
        strips[g, piece:, :piece] = jnp.zeros((piece, piece), BF16)
        strips[g, piece:, piece:] = strip[:, : length - piece]

    channel = lax.broadcasted_iota(jnp.int32, (1, width), 1) // CPG
    picks = [jnp.where(channel == g, 1.0, 0.0).astype(BF16) for g in range(groups)]

    for step in range(1, n):
        inward(lax.rem(me + step, n)).wait_recv()

    for block in range(n):
        rows = slice(block * piece, (block + 1) * piece)
        signal = recv[n - 1 - block, :, :width]
        grads = recv[block, :, width:]
        for g in range(groups):
            masked[g, rows, :width] = signal * picks[g]
            masked[g, rows, width:] = grads * picks[g]

    def give(block, values, staged, landed, out_sem, in_sem):
        def copy():
            return pltpu.make_async_remote_copy(
                src_ref=staged.at[block], dst_ref=landed.at[me],
                send_sem=out_sem.at[block], recv_sem=in_sem.at[me],
                device_id={"ctx": jnp.int32(block)}, device_id_type=MESH,
            )

        @pl.when(me == block)
        def _():
            landed[me] = values

        @pl.when(me != block)
        def _():
            staged[block] = values
            copy().start()

    for pair in range(n // 2):
        first = 2 * pair * piece
        total = dot(strips[0, :, : length - first], masked[0, first:, :])
        for g in range(1, groups):
            total += dot(strips[g, :, : length - first], masked[g, first:, :])
        total = total.astype(BF16)
        for half in range(2):
            rows = slice(half * piece, (half + 1) * piece)
            block = 2 * pair + half
            give(n - 1 - block, total[rows, :width], retc, backc, csend_sem, crecv_sem)
            give(block, total[rows, width:], reta, backa, asend_sem, arecv_sem)

    for block in range(n):
        span = slice(block * width, (block + 1) * width)
        for g in range(groups):
            lhs[g * piece : (g + 1) * piece, span] = recv[block, :, :width] * picks[g]
        rhs[:piece, span] = recv[block, :, width:]
        if block + 1 < n:
            rhs[piece:, span] = recv[block + 1, :, width:]
        else:
            rhs[piece:, span] = jnp.zeros((piece, width), BF16)
    lags[:, length:] = jnp.zeros((groups * piece, piece), F32)
    for pair in range(n // 2):
        first = 2 * pair * piece
        depth = (n - 2 * pair) * width
        lags[:, first : first + 2 * piece] = dot(
            lhs[:, :depth], rhs[:, 2 * pair * width :], ((1,), (1,))
        )
    for g in range(groups):
        skewed = pltpu.roll(lags[g * piece : (g + 1) * piece, :], 1, 1, stride=1, stride_axis=0)
        sums = jnp.sum(skewed, axis=0, keepdims=True)[:, piece:] * F32(scale)
        for to in range(ndp):
            gsend[to, g : g + 1, :] = sums[:, to * part : (to + 1) * part]

    def terms(to, at):
        return pltpu.make_async_remote_copy(
            src_ref=gsend.at[to], dst_ref=grecv.at[at],
            send_sem=gsend_sem.at[to], recv_sem=grecv_sem.at[at],
            device_id={"dp": to}, device_id_type=MESH,
        )

    for step in range(1, ndp):
        terms(lax.rem(row + step, ndp), row).start()
    grecv[row] = gsend[row]

    for owner in range(n):
        span = slice(owner * width, (owner + 1) * width)

        @pl.when(me != owner)
        def _():
            pltpu.make_async_remote_copy(
                src_ref=retc.at[owner], dst_ref=backc.at[owner],
                send_sem=csend_sem.at[owner], recv_sem=crecv_sem.at[owner],
                device_id={"ctx": jnp.int32(owner)}, device_id_type=MESH,
            ).wait()
            pltpu.make_async_remote_copy(
                src_ref=reta.at[owner], dst_ref=backa.at[owner],
                send_sem=asend_sem.at[owner], recv_sem=arecv_sem.at[owner],
                device_id={"ctx": jnp.int32(owner)}, device_id_type=MESH,
            ).wait()

        conv_ref[:, span] = dot(flip, backc[owner]).astype(BF16)
        adj_ref[:, span] = backa[owner]

    for step in range(1, ndp):
        other = lax.rem(row + step, ndp)
        terms(other, other).wait()
    gathered = grecv[0]
    for at in range(1, ndp):
        gathered += grecv[at]
    gf_ref[...] = gathered

    for step in range(1, n):
        outward(step).wait_send()


def solution(mesh):
    n, ndp = mesh.shape["ctx"], mesh.shape["dp"]

    def local(query, key_in, value, cotangent, filters):
        count, piece, channels = query.shape
        groups, length = filters.shape
        width = channels // n
        part = length // ndp
        scale = 1.0 / math.sqrt(count * ndp * length * CPG)
        q, k, v, ct = (x.reshape(piece, channels) for x in (query, key_in, value, cotangent))
        vmem = pl.BlockSpec(memory_space=pltpu.VMEM)
        dma = pltpu.SemaphoreType.DMA
        conv, adjoint, grad_filter = pl.pallas_call(
            functools.partial(kernel, n, ndp, scale),
            out_shape=(
                jax.ShapeDtypeStruct((piece, channels), BF16),
                jax.ShapeDtypeStruct((piece, channels), BF16),
                jax.ShapeDtypeStruct((groups, part), F32),
            ),
            in_specs=[vmem] * 5,
            out_specs=(vmem, vmem, vmem),
            scratch_shapes=[
                pltpu.VMEM((n, piece, 2 * width), BF16),
                pltpu.VMEM((n, piece, 2 * width), BF16),
                pltpu.VMEM((groups, 2 * piece, length), BF16),
                pltpu.VMEM((groups, length, 2 * width), BF16),
                pltpu.VMEM((n, piece, width), BF16),
                pltpu.VMEM((n, piece, width), BF16),
                pltpu.VMEM((n, piece, width), BF16),
                pltpu.VMEM((n, piece, width), BF16),
                pltpu.VMEM((groups * piece, n * width), BF16),
                pltpu.VMEM((2 * piece, n * width), BF16),
                pltpu.VMEM((groups * piece, length + piece), F32),
                pltpu.VMEM((ndp, groups, part), F32),
                pltpu.VMEM((ndp, groups, part), F32),
                dma((n,)), dma((n,)), dma((n,)), dma((n,)), dma((n,)), dma((n,)),
                dma((ndp,)), dma((ndp,)),
            ],
            compiler_params=pltpu.CompilerParams(
                collective_id=0, has_side_effects=True, vmem_limit_bytes=40 * 1024 * 1024
            ),
            cost_estimate=pl.CostEstimate(
                flops=3 * channels * length * length // n,
                bytes_accessed=12 * piece * channels,
                transcendentals=0,
            ),
        )(q, k, v, ct, filters)
        conv = conv.reshape(query.shape).astype(F32)
        adjoint = adjoint.reshape(query.shape).astype(F32)
        output = (query.astype(F32) * conv).astype(BF16)
        grad_query = (cotangent.astype(F32) * conv).astype(BF16)
        grad_key = (adjoint * value.astype(F32)).astype(BF16)
        grad_value = (adjoint * key_in.astype(F32)).astype(BF16)
        return output, grad_query, grad_key, grad_value, grad_filter

    signal = P("dp", "ctx", None)
    return jax.shard_map(
        local,
        mesh=mesh,
        in_specs=(signal, signal, signal, signal, P("ctx", None)),
        out_specs=(signal, signal, signal, signal, P("ctx", "dp")),
        check_vma=False,
    )
```

```python
import functools
import math

import jax
import jax.numpy as jnp
from jax import lax
from jax.experimental import pallas as pl
from jax.experimental.pallas import tpu as pltpu
from jax.sharding import PartitionSpec as P

CPG = 32
MESH = pl.DeviceIdType.MESH
F32 = jnp.float32
BF16 = jnp.bfloat16


def dot(a, b, contract=((1,), (0,))):
    return lax.dot_general(a, b, (contract, ((), ())), preferred_element_type=F32)


def kernel(
    n, ndp, scale,
    q_hbm, k_hbm, v_hbm, ct_hbm, f_hbm,
    conv_ref, adj_ref, gf_ref,
    q_ref, k_ref, v_ref, ct_ref, f_ref, load_sem,
    slong, sshort, rlong, rshort, rcross, fpair, strips, mlong, mshort,
    tlong, tshort, backl, backs, lhs, rhs, lags, gsend, grecv,
    slong_sem, sshort_sem, scross_sem, rlong_sem, rshort_sem, rcross_sem, f_sem,
    tlong_sem, tshort_sem, backl_sem, backs_sem, gsend_sem, grecv_sem,
):
    me = lax.axis_index("ctx")
    row = lax.axis_index("dp")
    hn = n // 2
    half = me // hn
    rank = me - half * hn
    partner = (1 - half) * hn + rank
    low = half == 0
    piece, channels = q_ref.shape
    width = channels // n
    groups, length = f_ref.shape
    part = length // ndp
    reach = hn * piece
    long_slot = (1 - half) * rank + half * (hn - 1 - rank)
    short_slot = hn - 1 - long_slot

    def choose(a, b):
        return jnp.where(low, a.astype(F32), b.astype(F32)).astype(BF16)

    loads = [
        pltpu.make_async_copy(hbm, ref, load_sem.at[at])
        for at, (hbm, ref) in enumerate(
            [(k_hbm, k_ref), (v_hbm, v_ref), (ct_hbm, ct_ref), (q_hbm, q_ref), (f_hbm, f_ref)]
        )
    ]
    for load in loads:
        load.start()
    barrier = pltpu.get_barrier_semaphore()
    for step in range(1, n):
        pl.semaphore_signal(
            barrier, inc=1, device_id={"ctx": lax.rem(me + step, n)}, device_id_type=MESH
        )
    for step in range(1, ndp):
        to = lax.rem(row + step, ndp)
        pl.semaphore_signal(barrier, inc=1, device_id={"dp": to}, device_id_type=MESH)
        pl.semaphore_signal(
            barrier, inc=1, device_id={"ctx": partner, "dp": to}, device_id_type=MESH
        )

    at_row = lax.broadcasted_iota(jnp.int32, (piece, piece), 0)
    at_col = lax.broadcasted_iota(jnp.int32, (piece, piece), 1)
    flip = jnp.where(at_row + at_col == piece - 1, 1.0, 0.0).astype(BF16)

    loads[0].wait()
    loads[1].wait()
    mixed = (k_ref[...].astype(F32) * v_ref[...].astype(F32)).astype(BF16)
    turned = dot(flip, mixed).astype(BF16)
    loads[2].wait()
    loads[3].wait()
    gradin = (ct_ref[...].astype(F32) * q_ref[...].astype(F32)).astype(BF16)
    long = choose(gradin, turned)
    short = choose(turned, gradin)
    for owner in range(hn):
        for block in range(2):
            to = slice(block * width, (block + 1) * width)
            at = (owner + block * hn) * width
            slong[owner, :, to] = long[:, at : at + width]
            sshort[owner, :, to] = short[:, at : at + width]
    loads[4].wait()
    fpair[half] = f_ref[...].astype(F32)
    pl.semaphore_wait(barrier, n - 1 + 2 * (ndp - 1))

    def copy(src, dst, out_sem, in_sem, to):
        return pltpu.make_async_remote_copy(
            src_ref=src, dst_ref=dst, send_sem=out_sem, recv_sem=in_sem,
            device_id={"ctx": to}, device_id_type=MESH,
        )

    filters_copy = copy(fpair.at[half], fpair.at[half], f_sem.at[0], f_sem.at[1], partner)
    filters_copy.start()
    outward = []
    for step in range(1, hn):
        owner = lax.rem(rank + step, hn)
        outward.append(copy(
            sshort.at[owner], rshort.at[short_slot], sshort_sem.at[owner],
            rshort_sem.at[short_slot], half * hn + owner,
        ))
    for step in range(hn):
        owner = lax.rem(rank + step, hn)
        outward.append(copy(
            sshort.at[owner], rcross.at[short_slot], scross_sem.at[owner],
            rcross_sem.at[short_slot], (1 - half) * hn + owner,
        ))
    for step in range(1, hn):
        owner = lax.rem(rank + step, hn)
        outward.append(copy(
            slong.at[owner], rlong.at[long_slot], slong_sem.at[owner],
            rlong_sem.at[long_slot], half * hn + owner,
        ))
    for each in outward:
        each.start()
    rlong[long_slot] = slong[rank]
    rshort[short_slot] = sshort[rank]

    copy(
        fpair.at[1 - half], fpair.at[1 - half], f_sem.at[0], f_sem.at[1], partner
    ).wait_recv()
    for g in range(2 * groups):
        line = fpair[g // groups, g % groups : g % groups + 1, :]
        line = jnp.concatenate([line, jnp.zeros((1, piece), F32)], axis=1)
        spread = jnp.broadcast_to(line, (piece, length + piece))
        strip = pltpu.roll(spread, 0, 1, stride=1, stride_axis=0).astype(BF16)
        strips[g, :piece] = strip[:, :length]
        strips[g, piece:, :piece] = jnp.zeros((piece, piece), BF16)
        strips[g, piece:, piece:] = strip[:, : length - piece]

    channel = lax.broadcasted_iota(jnp.int32, (1, width), 1) // CPG
    picks = [jnp.where(channel == g, 1.0, 0.0).astype(BF16) for g in range(groups)]

    def arrive(landed, sem, slot):
        copy(landed.at[slot], landed.at[slot], slong_sem.at[0], sem.at[slot], partner).wait_recv()

    def spread_out(landed, slot, masked, at):
        for g in range(2 * groups):
            side = (g // groups) * width
            masked[g, at * piece : (at + 1) * piece, :] = (
                landed[slot, :, side : side + width] * picks[g % groups]
            )

    def convolve(masked, depth, staged, landed, out_sem, in_sem, own_slot, mirrored):
        for pair in range(hn // 2):
            first = 2 * pair * piece
            for block in range(2):
                total = None
                for g in range(block * groups, (block + 1) * groups):
                    term = dot(strips[g, :, : depth - first], masked[g, first:, :])
                    total = term if total is None else total + term
                total = total.astype(BF16)
                for at in range(2):
                    staged[2 * pair + at, :, block * width : (block + 1) * width] = total[
                        at * piece : (at + 1) * piece
                    ]
            for at in range(2):
                slot = 2 * pair + at
                source = mirrored * (hn - 1 - slot) + (1 - mirrored) * slot

                @pl.when(own_slot == slot)
                def _():
                    landed[rank] = staged[slot]

                @pl.when(own_slot != slot)
                def _():
                    copy(
                        staged.at[slot], landed.at[rank], out_sem.at[slot], in_sem.at[rank],
                        half * hn + source,
                    ).start()

    for slot in range(hn):
        @pl.when(slot != short_slot)
        def _():
            arrive(rshort, rshort_sem, slot)
        spread_out(rshort, slot, mshort, slot)
    convolve(mshort, reach, tshort, backs, tshort_sem, backs_sem, short_slot, 1 - half)

    for slot in range(hn):
        arrive(rcross, rcross_sem, slot)
        spread_out(rcross, slot, mlong, hn + slot)
    for slot in range(hn):
        @pl.when(slot != long_slot)
        def _():
            arrive(rlong, rlong_sem, slot)
        spread_out(rlong, slot, mlong, slot)
    convolve(mlong, 2 * reach, tlong, backl, tlong_sem, backl_sem, long_slot, half)

    def lanes(values, role):
        left, right = values[:, :width], values[:, width:]
        return choose(left, right) if role == 0 else choose(right, left)

    def fill(at, values):
        rhs[:piece, at * width : (at + 1) * width] = values
        if at > 0:
            rhs[piece:, (at - 1) * width : at * width] = values

    def fill_lhs(at, values):
        for g in range(groups):
            lhs[g * piece : (g + 1) * piece, at * width : (at + 1) * width] = values * picks[g]

    none = jnp.zeros((piece, width), BF16)

    def lag_sums(g, extent):
        rows = slice(g * piece, (g + 1) * piece)
        skewed = pltpu.roll(lags[rows, : extent + piece], 1, 1, stride=1, stride_axis=0)
        return jnp.sum(skewed, axis=0, keepdims=True)[:, piece:] * F32(scale)

    def keep(role, g, sums, extent):
        for to in range(ndp):
            if to * part < extent:
                gsend[role, to, g : g + 1, :] = sums[:, to * part : (to + 1) * part]
            else:
                gsend[role, to, g : g + 1, :] = jnp.zeros((1, part), F32)

    def terms(role, to, at):
        return pltpu.make_async_remote_copy(
            src_ref=gsend.at[role, to], dst_ref=grecv.at[role, at],
            send_sem=gsend_sem.at[role, to], recv_sem=grecv_sem.at[role, at],
            device_id={"ctx": me if role == 0 else partner, "dp": to}, device_id_type=MESH,
        )

    for role in (1, 0):
        for at in range(hn):
            fill_lhs(at, lanes(choose(rshort[hn - 1 - at], rlong[hn - 1 - at]), role))
            fill(at, lanes(choose(rlong[at], rshort[at]), role))
        fill(hn, none)
        for pair in range(hn // 2):
            first = 2 * pair
            lags[:, first * piece : (first + 2) * piece] = dot(
                lhs[:, : (hn - first) * width], rhs[:, first * width : hn * width], ((1,), (1,))
            )
        if role == 1:
            lags[:, reach : reach + piece] = jnp.zeros((groups * piece, piece), F32)
            for g in range(groups):
                keep(1, g, lag_sums(g, reach), reach)
            for step in range(ndp):
                to = lax.rem(row + step, ndp)
                terms(1, to, row).start()
    for at in range(hn):
        fill_lhs(at, lanes(choose(rshort[hn - 1 - at], rcross[hn - 1 - at]), 0))
    for at in range(n + hn):
        if hn <= at < n:
            fill(at, lanes(choose(rcross[at - hn], rshort[at - hn]), 0))
        else:
            fill(at, none)
    fill_last = slice((n + hn - 1) * width, (n + hn) * width)
    rhs[piece:, fill_last] = none
    lags[:, reach:] = jnp.zeros((groups * piece, length - reach + piece), F32)
    for pair in range(hn):
        first = 2 * pair
        lags[:, first * piece : (first + 2) * piece] += dot(
            lhs[...], rhs[:, first * width : (first + hn) * width], ((1,), (1,))
        )
    for g in range(groups):
        keep(0, g, lag_sums(g, length), length)
    for step in range(1, ndp):
        terms(0, lax.rem(row + step, ndp), row).start()
    grecv[0, row] = gsend[0, row]

    for owner in range(hn):
        @pl.when(rank != owner)
        def _():
            arrive(backs, backs_sem, owner)
            arrive(backl, backl_sem, owner)
        conv = dot(flip, choose(backs[owner], backl[owner])).astype(BF16)
        adjoint = choose(backl[owner], backs[owner])
        for block in range(2):
            side = slice(block * width, (block + 1) * width)
            at = (owner + block * hn) * width
            conv_ref[:, at : at + width] = conv[:, side]
            adj_ref[:, at : at + width] = adjoint[:, side]

    for step in range(1, ndp):
        other = lax.rem(row + step, ndp)
        terms(0, other, other).wait()
    for step in range(ndp):
        other = lax.rem(row + step, ndp)
        terms(1, other, other).wait()
    gathered = grecv[0, 0]
    for at in range(1, 2 * ndp):
        gathered += grecv[at // ndp, at % ndp]
    gf_ref[...] = gathered

    filters_copy.wait_send()
    for each in outward:
        each.wait_send()
    for slot in range(hn):
        @pl.when(slot != short_slot)
        def _():
            copy(
                tshort.at[slot], backs.at[rank], tshort_sem.at[slot], backs_sem.at[rank], partner
            ).wait_send()

        @pl.when(slot != long_slot)
        def _():
            copy(
                tlong.at[slot], backl.at[rank], tlong_sem.at[slot], backl_sem.at[rank], partner
            ).wait_send()


def solution(mesh):
    n, ndp = mesh.shape["ctx"], mesh.shape["dp"]

    def local(query, key_in, value, cotangent, filters):
        count, piece, channels = query.shape
        groups, length = filters.shape
        hn, width = n // 2, channels // n
        part = length // ndp
        scale = 1.0 / math.sqrt(count * ndp * length * CPG)
        q, k, v, ct = (x.reshape(piece, channels) for x in (query, key_in, value, cotangent))
        vmem = pl.BlockSpec(memory_space=pltpu.VMEM)
        dma = pltpu.SemaphoreType.DMA
        conv, adjoint, grad_filter = pl.pallas_call(
            functools.partial(kernel, n, ndp, scale),
            out_shape=(
                jax.ShapeDtypeStruct((piece, channels), BF16),
                jax.ShapeDtypeStruct((piece, channels), BF16),
                jax.ShapeDtypeStruct((groups, part), F32),
            ),
            in_specs=[pl.BlockSpec(memory_space=pltpu.HBM)] * 5,
            out_specs=(vmem, vmem, vmem),
            scratch_shapes=[
                pltpu.VMEM((piece, channels), BF16),
                pltpu.VMEM((piece, channels), BF16),
                pltpu.VMEM((piece, channels), BF16),
                pltpu.VMEM((piece, channels), BF16),
                pltpu.VMEM((groups, length), BF16),
                dma((5,)),
                *[pltpu.VMEM((hn, piece, 2 * width), BF16) for _ in range(5)],
                pltpu.VMEM((2, groups, length), F32),
                pltpu.VMEM((2 * groups, 2 * piece, length), BF16),
                pltpu.VMEM((2 * groups, length, width), BF16),
                pltpu.VMEM((2 * groups, length // 2, width), BF16),
                *[pltpu.VMEM((hn, piece, 2 * width), BF16) for _ in range(4)],
                pltpu.VMEM((groups * piece, hn * width), BF16),
                pltpu.VMEM((2 * piece, (n + hn) * width), BF16),
                pltpu.VMEM((groups * piece, length + piece), F32),
                pltpu.VMEM((2, ndp, groups, part), F32),
                pltpu.VMEM((2, ndp, groups, part), F32),
                *[dma((hn,)) for _ in range(6)],
                dma((2,)),
                *[dma((hn,)) for _ in range(4)],
                dma((2, ndp)), dma((2, ndp)),
            ],
            compiler_params=pltpu.CompilerParams(
                collective_id=0, has_side_effects=True, vmem_limit_bytes=40 * 1024 * 1024
            ),
            cost_estimate=pl.CostEstimate(
                flops=3 * channels * length * length // n,
                bytes_accessed=12 * piece * channels,
                transcendentals=0,
            ),
        )(q, k, v, ct, filters)
        conv = conv.reshape(query.shape).astype(F32)
        adjoint = adjoint.reshape(query.shape).astype(F32)
        output = (query.astype(F32) * conv).astype(BF16)
        grad_query = (cotangent.astype(F32) * conv).astype(BF16)
        grad_key = (adjoint * value.astype(F32)).astype(BF16)
        grad_value = (adjoint * key_in.astype(F32)).astype(BF16)
        return output, grad_query, grad_key, grad_value, grad_filter

    signal = P("dp", "ctx", None)
    return jax.shard_map(
        local,
        mesh=mesh,
        in_specs=(signal, signal, signal, signal, P("ctx", None)),
        out_specs=(signal, signal, signal, signal, P("ctx", "dp")),
        check_vma=False,
    )
```

```python
import functools
import math

import jax
import jax.numpy as jnp
from jax import lax
from jax.experimental import pallas as pl
from jax.experimental.pallas import tpu as pltpu
from jax.sharding import PartitionSpec as P

CPG = 32
STEPS = 2
MESH = pl.DeviceIdType.MESH
F32 = jnp.float32
BF16 = jnp.bfloat16


def dot(a, b, contract=((1,), (0,))):
    return lax.dot_general(a, b, (contract, ((), ())), preferred_element_type=F32)


def kernel(
    n, ndp, scale,
    q_hbm, k_hbm, v_hbm, ct_hbm, f_hbm,
    conv_ref, adj_ref, gf_ref,
    q_ref, k_ref, v_ref, ct_ref, f_ref, load_sem,
    slong, sshort, rlong, rshort, rcross, fpair, strips, crossed, mlong, mshort,
    tlong, tshort, backl, backs, lhs, rhs, lags, gsend, grecv,
    slong_sem, sshort_sem, scross_sem, rlong_sem, rshort_sem, rcross_sem, f_sem,
    tlong_sem, tshort_sem, backl_sem, backs_sem, gsend_sem, grecv_sem,
):
    me = lax.axis_index("ctx")
    row = lax.axis_index("dp")
    hn = n // 2
    half = me // hn
    rank = me - half * hn
    partner = (1 - half) * hn + rank
    low = half == 0
    piece, channels = q_ref.shape
    width = channels // n
    groups, length = f_ref.shape
    part = length // ndp
    reach = hn * piece
    long_slot = (1 - half) * rank + half * (hn - 1 - rank)
    short_slot = hn - 1 - long_slot

    def choose(a, b):
        return jnp.where(low, a.astype(F32), b.astype(F32)).astype(BF16)

    loads = [
        pltpu.make_async_copy(hbm, ref, load_sem.at[at])
        for at, (hbm, ref) in enumerate(
            [(k_hbm, k_ref), (v_hbm, v_ref), (ct_hbm, ct_ref), (q_hbm, q_ref), (f_hbm, f_ref)]
        )
    ]
    for load in loads:
        load.start()
    barrier = pltpu.get_barrier_semaphore()
    for step in range(1, n):
        pl.semaphore_signal(
            barrier, inc=1, device_id={"ctx": lax.rem(me + step, n)}, device_id_type=MESH
        )
    for step in range(1, ndp):
        to = lax.rem(row + step, ndp)
        pl.semaphore_signal(barrier, inc=1, device_id={"dp": to}, device_id_type=MESH)
        pl.semaphore_signal(
            barrier, inc=1, device_id={"ctx": partner, "dp": to}, device_id_type=MESH
        )

    at_row = lax.broadcasted_iota(jnp.int32, (piece, piece), 0)
    at_col = lax.broadcasted_iota(jnp.int32, (piece, piece), 1)
    flip = jnp.where(at_row + at_col == piece - 1, 1.0, 0.0).astype(BF16)

    def gate_mixed(staged):
        loads[0].wait()
        loads[1].wait()
        mixed = (k_ref[...].astype(F32) * v_ref[...].astype(F32)).astype(BF16)
        stage(staged, dot(flip, mixed).astype(BF16))

    def gate_gradin(staged):
        loads[2].wait()
        loads[3].wait()
        stage(staged, (ct_ref[...].astype(F32) * q_ref[...].astype(F32)).astype(BF16))

    def stage(staged, values):
        for owner in range(hn):
            for block in range(2):
                at = (owner + block * hn) * width
                staged[owner, :, block * width : (block + 1) * width] = values[:, at : at + width]

    @pl.when(half == 0)
    def _():
        gate_mixed(sshort)

    @pl.when(half != 0)
    def _():
        gate_gradin(sshort)

    loads[4].wait()
    fpair[half] = f_ref[...].astype(F32)
    pl.semaphore_wait(barrier, n - 1 + 2 * (ndp - 1))

    def copy(src, dst, out_sem, in_sem, to):
        return pltpu.make_async_remote_copy(
            src_ref=src, dst_ref=dst, send_sem=out_sem, recv_sem=in_sem,
            device_id={"ctx": to}, device_id_type=MESH,
        )

    filters_copy = copy(fpair.at[half], fpair.at[half], f_sem.at[0], f_sem.at[1], partner)
    filters_copy.start()
    outward = []
    for step in range(1, hn):
        owner = lax.rem(rank + step, hn)
        outward.append(copy(
            sshort.at[owner], rshort.at[short_slot], sshort_sem.at[owner],
            rshort_sem.at[short_slot], half * hn + owner,
        ))
    for step in range(hn):
        owner = lax.rem(rank + step, hn)
        outward.append(copy(
            sshort.at[owner], rcross.at[short_slot], scross_sem.at[owner],
            rcross_sem.at[short_slot], (1 - half) * hn + owner,
        ))
    for each in outward:
        each.start()
    rshort[short_slot] = sshort[rank]

    @pl.when(half == 0)
    def _():
        gate_gradin(slong)

    @pl.when(half != 0)
    def _():
        gate_mixed(slong)

    later = []
    for step in range(1, hn):
        owner = lax.rem(rank + step, hn)
        later.append(copy(
            slong.at[owner], rlong.at[long_slot], slong_sem.at[owner],
            rlong_sem.at[long_slot], half * hn + owner,
        ))
    for each in later:
        each.start()
    rlong[long_slot] = slong[rank]

    copy(
        fpair.at[1 - half], fpair.at[1 - half], f_sem.at[0], f_sem.at[1], partner
    ).wait_recv()
    for g in range(2 * groups):
        line = fpair[g // groups, g % groups : g % groups + 1, :]
        line = jnp.concatenate([line, jnp.zeros((1, piece), F32)], axis=1)
        spread = jnp.broadcast_to(line, (piece, length + piece))
        strip = pltpu.roll(spread, 0, 1, stride=1, stride_axis=0).astype(BF16)
        strips[g, :piece] = strip[:, :length]
        strips[g, piece:, :piece] = jnp.zeros((piece, piece), BF16)
        strips[g, piece:, piece:] = strip[:, : length - piece]

    channel = lax.broadcasted_iota(jnp.int32, (1, width), 1) // CPG
    picks = [jnp.where(channel == g, 1.0, 0.0).astype(BF16) for g in range(groups)]

    def arrive(landed, sem, slot):
        copy(landed.at[slot], landed.at[slot], slong_sem.at[0], sem.at[slot], partner).wait_recv()

    def spread_out(landed, slot, masked, at):
        for g in range(2 * groups):
            side = (g // groups) * width
            masked[g, at * piece : (at + 1) * piece, :] = (
                landed[slot, :, side : side + width] * picks[g % groups]
            )

    def convolve(masked, beyond, staged, landed, out_sem, in_sem, own_slot, mirrored):
        for pair in range(hn // 2):
            first = 2 * pair * piece
            for block in range(2):
                span = slice(block * width, (block + 1) * width)
                total = None if beyond is None else beyond[first : first + 2 * piece, span]
                for g in range(block * groups, (block + 1) * groups):
                    term = dot(strips[g, :, : reach - first], masked[g, first:reach, :])
                    total = term if total is None else total + term
                total = total.astype(BF16)
                for at in range(2):
                    staged[2 * pair + at, :, span] = total[at * piece : (at + 1) * piece]
            for at in range(2):
                slot = 2 * pair + at
                source = mirrored * (hn - 1 - slot) + (1 - mirrored) * slot

                @pl.when(own_slot == slot)
                def _():
                    landed[rank] = staged[slot]

                @pl.when(own_slot != slot)
                def _():
                    copy(
                        staged.at[slot], landed.at[rank], out_sem.at[slot], in_sem.at[rank],
                        half * hn + source,
                    ).start()

    for slot in range(hn):
        @pl.when(slot != short_slot)
        def _():
            arrive(rshort, rshort_sem, slot)
        spread_out(rshort, slot, mshort, slot)
    convolve(mshort, None, tshort, backs, tshort_sem, backs_sem, short_slot, 1 - half)

    for slot in range(hn):
        arrive(rcross, rcross_sem, slot)
        spread_out(rcross, slot, mlong, hn + slot)
    for pair in range(hn // 2):
        first = 2 * pair * piece
        for block in range(2):
            total = None
            for g in range(block * groups, (block + 1) * groups):
                term = dot(strips[g, :, reach - first : length - first], mlong[g, reach:, :])
                total = term if total is None else total + term
            crossed[first : first + 2 * piece, block * width : (block + 1) * width] = total
    for slot in range(hn):
        @pl.when(slot != long_slot)
        def _():
            arrive(rlong, rlong_sem, slot)
        spread_out(rlong, slot, mlong, slot)
    convolve(mlong, crossed, tlong, backl, tlong_sem, backl_sem, long_slot, half)

    def lanes(values, role):
        left, right = values[:, :width], values[:, width:]
        return choose(left, right) if role == 0 else choose(right, left)

    def fill(at, values):
        rhs[:piece, at * width : (at + 1) * width] = values
        if at > 0:
            rhs[piece:, (at - 1) * width : at * width] = values

    def fill_lhs(at, values):
        for g in range(groups):
            lhs[g * piece : (g + 1) * piece, at * width : (at + 1) * width] = values * picks[g]

    none = jnp.zeros((piece, width), BF16)

    def lag_sums(g, extent):
        rows = slice(g * piece, (g + 1) * piece)
        skewed = pltpu.roll(lags[rows, : extent + piece], 1, 1, stride=1, stride_axis=0)
        return jnp.sum(skewed, axis=0, keepdims=True)[:, piece:] * F32(scale)

    def keep(role, g, sums, extent):
        for to in range(ndp):
            if to * part < extent:
                gsend[role, to, g : g + 1, :] = sums[:, to * part : (to + 1) * part]
            else:
                gsend[role, to, g : g + 1, :] = jnp.zeros((1, part), F32)

    def terms(role, to, at):
        return pltpu.make_async_remote_copy(
            src_ref=gsend.at[role, to], dst_ref=grecv.at[role, at],
            send_sem=gsend_sem.at[role, to], recv_sem=grecv_sem.at[role, at],
            device_id={"ctx": me if role == 0 else partner, "dp": to}, device_id_type=MESH,
        )

    for role in (1, 0):
        for at in range(hn):
            fill_lhs(at, lanes(choose(rshort[hn - 1 - at], rlong[hn - 1 - at]), role))
            fill(at, lanes(choose(rlong[at], rshort[at]), role))
        fill(hn, none)
        for pair in range(hn // 2):
            first = 2 * pair
            lags[:, first * piece : (first + 2) * piece] = dot(
                lhs[:, : (hn - first) * width], rhs[:, first * width : hn * width], ((1,), (1,))
            )
        if role == 1:
            lags[:, reach : reach + piece] = jnp.zeros((groups * piece, piece), F32)
            for g in range(groups):
                keep(1, g, lag_sums(g, reach), reach)
            for step in range(ndp):
                to = lax.rem(row + step, ndp)
                terms(1, to, row).start()
    for at in range(hn):
        fill_lhs(at, lanes(choose(rshort[hn - 1 - at], rcross[hn - 1 - at]), 0))
    for at in range(n + hn):
        if hn <= at < n:
            fill(at, lanes(choose(rcross[at - hn], rshort[at - hn]), 0))
        else:
            fill(at, none)
    fill_last = slice((n + hn - 1) * width, (n + hn) * width)
    rhs[piece:, fill_last] = none
    lags[:, reach:] = jnp.zeros((groups * piece, length - reach + piece), F32)
    for pair in range(hn):
        first = 2 * pair
        lags[:, first * piece : (first + 2) * piece] += dot(
            lhs[...], rhs[:, first * width : (first + hn) * width], ((1,), (1,))
        )
    for g in range(groups):
        keep(0, g, lag_sums(g, length), length)
    for step in range(1, ndp):
        terms(0, lax.rem(row + step, ndp), row).start()
    grecv[0, row] = gsend[0, row]

    for owner in range(hn):
        @pl.when(rank != owner)
        def _():
            arrive(backs, backs_sem, owner)
            arrive(backl, backl_sem, owner)
        conv = dot(flip, choose(backs[owner], backl[owner])).astype(BF16)
        adjoint = choose(backl[owner], backs[owner])
        for block in range(2):
            side = slice(block * width, (block + 1) * width)
            at = (owner + block * hn) * width
            conv_ref[:, at : at + width] = conv[:, side]
            adj_ref[:, at : at + width] = adjoint[:, side]

    for step in range(1, ndp):
        other = lax.rem(row + step, ndp)
        terms(0, other, other).wait()
    for step in range(ndp):
        other = lax.rem(row + step, ndp)
        terms(1, other, other).wait()
    gathered = grecv[0, 0]
    for at in range(1, 2 * ndp):
        gathered += grecv[at // ndp, at % ndp]
    gf_ref[...] = gathered

    filters_copy.wait_send()
    for each in outward + later:
        each.wait_send()
    for slot in range(hn):
        @pl.when(slot != short_slot)
        def _():
            copy(
                tshort.at[slot], backs.at[rank], tshort_sem.at[slot], backs_sem.at[rank], partner
            ).wait_send()

        @pl.when(slot != long_slot)
        def _():
            copy(
                tlong.at[slot], backl.at[rank], tlong_sem.at[slot], backl_sem.at[rank], partner
            ).wait_send()


def finish(q, k, v, ct, conv, adjoint, gf, output, grad_q, grad_k, grad_v, grad_f):
    conv_wide, adjoint_wide = conv[...].astype(F32), adjoint[...].astype(F32)
    output[...] = (q[...].astype(F32) * conv_wide).astype(BF16)
    grad_q[...] = (ct[...].astype(F32) * conv_wide).astype(BF16)
    grad_k[...] = (adjoint_wide * v[...].astype(F32)).astype(BF16)
    grad_v[...] = (adjoint_wide * k[...].astype(F32)).astype(BF16)
    grad_f[...] = gf[...]


def solution(mesh):
    n, ndp = mesh.shape["ctx"], mesh.shape["dp"]

    def local(query, key_in, value, cotangent, filters):
        count, piece, channels = query.shape
        groups, length = filters.shape
        hn, width = n // 2, channels // n
        part = length // ndp
        scale = 1.0 / math.sqrt(count * ndp * length * CPG)
        q, k, v, ct = (x.reshape(piece, channels) for x in (query, key_in, value, cotangent))
        vmem = pl.BlockSpec(memory_space=pltpu.VMEM)
        dma = pltpu.SemaphoreType.DMA
        conv, adjoint, grad_filter = pl.pallas_call(
            functools.partial(kernel, n, ndp, scale),
            out_shape=(
                jax.ShapeDtypeStruct((piece, channels), BF16),
                jax.ShapeDtypeStruct((piece, channels), BF16),
                jax.ShapeDtypeStruct((groups, part), F32),
            ),
            in_specs=[pl.BlockSpec(memory_space=pltpu.HBM)] * 5,
            out_specs=(vmem, vmem, vmem),
            scratch_shapes=[
                pltpu.VMEM((piece, channels), BF16),
                pltpu.VMEM((piece, channels), BF16),
                pltpu.VMEM((piece, channels), BF16),
                pltpu.VMEM((piece, channels), BF16),
                pltpu.VMEM((groups, length), BF16),
                dma((5,)),
                *[pltpu.VMEM((hn, piece, 2 * width), BF16) for _ in range(5)],
                pltpu.VMEM((2, groups, length), F32),
                pltpu.VMEM((2 * groups, 2 * piece, length), BF16),
                pltpu.VMEM((hn * piece, 2 * width), F32),
                pltpu.VMEM((2 * groups, length, width), BF16),
                pltpu.VMEM((2 * groups, length // 2, width), BF16),
                *[pltpu.VMEM((hn, piece, 2 * width), BF16) for _ in range(4)],
                pltpu.VMEM((groups * piece, hn * width), BF16),
                pltpu.VMEM((2 * piece, (n + hn) * width), BF16),
                pltpu.VMEM((groups * piece, length + piece), F32),
                pltpu.VMEM((2, ndp, groups, part), F32),
                pltpu.VMEM((2, ndp, groups, part), F32),
                *[dma((hn,)) for _ in range(6)],
                dma((2,)),
                *[dma((hn,)) for _ in range(4)],
                dma((2, ndp)), dma((2, ndp)),
            ],
            compiler_params=pltpu.CompilerParams(
                collective_id=0, has_side_effects=True, vmem_limit_bytes=62 * 1024 * 1024
            ),
            cost_estimate=pl.CostEstimate(
                flops=3 * channels * length * length // n,
                bytes_accessed=12 * piece * channels,
                transcendentals=0,
            ),
        )(q, k, v, ct, filters)
        steps = STEPS if piece % (16 * STEPS) == 0 else 1
        rows = pl.BlockSpec((piece // steps, channels), lambda at: (at, 0))
        terms = pl.BlockSpec((groups, part), lambda at: (0, 0))
        gated = jax.ShapeDtypeStruct((piece, channels), BF16)
        *gated, grad_filter = pl.pallas_call(
            finish,
            grid=(steps,),
            out_shape=(gated, gated, gated, gated, jax.ShapeDtypeStruct((groups, part), F32)),
            in_specs=[rows] * 6 + [terms],
            out_specs=(rows, rows, rows, rows, terms),
            compiler_params=pltpu.CompilerParams(vmem_limit_bytes=62 * 1024 * 1024),
        )(q, k, v, ct, conv, adjoint, grad_filter)
        output, grad_query, grad_key, grad_value = (x.reshape(query.shape) for x in gated)
        return output, grad_query, grad_key, grad_value, grad_filter

    signal = P("dp", "ctx", None)
    return jax.shard_map(
        local,
        mesh=mesh,
        in_specs=(signal, signal, signal, signal, P("ctx", None)),
        out_specs=(signal, signal, signal, signal, P("ctx", "dp")),
        check_vma=False,
    )
```
